256 devices in a mesh: samp: 32 (over z, x), feat: 8 (over y, core).
Axes of the slice: x: 4, y: 4, z: 8, core: 2. Of those that a mesh axis runs over, the one named last changes fastest.
Arguments:
- features: float32 [32768, 16384], P('samp', 'feat'), as said below
- targets: float32 [32768, 64], P('samp'), may hold values from -6 to 6
- ridge: float32 [64], replicated, may hold values from 0.5 to 5
Outputs:
- solution: float32 [16384, 64], P('feat')
- residual: float32 [32768, 64], P('samp')
The draws below stay inside these ranges and needn't reach their ends.
Inputs may be any that keep to these rules, and one draw needn't show every extreme that they name: `features`: rows and columns carry independent positive scales; entries are finite.
All inputs are finite; a program needn't handle non-finite values.
Results may differ from the reference program's by a relative error of at most 0.0004.
Values sent between devices are 32-bit elements; how exact they have to be, the bound alone decides.
No kernel may reach another device: no remote copies, remote signals or barrier semaphores. Data moves between devices by JAX's collectives and lax.ppermute only.
A program may use at most 64 MiB of HBM per device.

```python
import math
import jax
import jax.numpy as jnp
from jax import lax

FEATURES = 16384
TARGETS = 64
ITERS = 3
SAMPLES = 32768


def draw_features(key, part):
    key = jax.random.fold_in(key, 11)
    key_rows, key_cols, key_body = jax.random.split(key, 3)
    row_scale = jnp.exp(jax.random.uniform(key_rows, (SAMPLES, 1), jnp.float32, 0.0, 2.302585))
    trend = 1.0 + 2.0 * jnp.arange(SAMPLES, dtype=jnp.float32)[:, None] / float(max(SAMPLES - 1, 1))
    col_scale = jnp.exp(jax.random.uniform(key_cols, (1, FEATURES), jnp.float32, 0.0, 2.302585))
    values = jax.random.normal(key_body, (SAMPLES, FEATURES), jnp.float32)
    scale = 0.2 / jnp.sqrt(jnp.float32(SAMPLES))
    return (values * row_scale * trend * col_scale * scale).astype(jnp.float32)


def level_of(key, dims, cuts, least, largest):
    def one(position, blocks):
        heights = jax.random.uniform(jax.random.fold_in(jax.random.fold_in(key, 6), position), (blocks,), jnp.float32, least / len(cuts), largest / len(cuts))
        return jnp.repeat(jnp.exp(heights), dims[position] // blocks).reshape((-1,) + (1,) * (len(dims) - position - 1))

    level = one(*cuts[0])
    for cut in cuts[1:]:
        level = level * one(*cut)
    return level


def gaussian(stream_key, extent, deviation, reach, cuts=(), kind=jnp.bfloat16):
    level = level_of(stream_key, extent, cuts, -0.22, 0.18) if cuts else 1.0
    drawn = jax.random.normal(stream_key, extent, jnp.float32) * deviation * level
    return jnp.minimum(jnp.maximum(drawn, -reach), reach).astype(kind)


def setup_inputs(seed: int = 0) -> dict:
    keys = jax.random.split(jax.random.key(seed), 4)
    return {
        "features": draw_features(jax.random.fold_in(keys[3], 71), 0),
        "targets": gaussian(keys[1], (SAMPLES, TARGETS), 1.0, 6.0, ((0, 32),), jnp.float32),
        "ridge": jnp.clip(jnp.exp(jax.random.uniform(keys[2], (TARGETS,), jnp.float32, math.log(0.5), math.log(5.0))), 0.5, 5.0),
    }


def reference(features, targets, ridge):
    high = lax.Precision.HIGHEST
    solution = jnp.zeros((features.shape[1], targets.shape[1]), jnp.float32)
    residual = targets
    gradient = lax.dot_general(features, residual, (((0,), (0,)), ((), ())), precision=high, preferred_element_type=jnp.float32)
    direction = gradient
    gamma = jnp.sum(gradient * gradient, axis=0)
    for step in range(ITERS):
        image = jnp.dot(features, direction, precision=high, preferred_element_type=jnp.float32)
        delta = jnp.sum(image * image, axis=0) + ridge * jnp.sum(direction * direction, axis=0)
        alpha = gamma / delta
        solution = solution + alpha * direction
        residual = residual - alpha * image
        if step + 1 < ITERS:
            gradient = lax.dot_general(features, residual, (((0,), (0,)), ((), ())), precision=high, preferred_element_type=jnp.float32) - ridge * solution
            fresh = jnp.sum(gradient * gradient, axis=0)
            direction = gradient + (fresh / gamma) * direction
            gamma = fresh
    return solution, residual
```

```python
import functools

import jax
import jax.numpy as jnp
from jax import lax
from jax.experimental import pallas as pl
from jax.experimental.pallas import tpu as pltpu
from jax.sharding import PartitionSpec as P

NZ, NX, NY, NC = 8, 4, 4, 2
Y_SHIFTS = [[(i, (i + NC * k) % (NY * NC)) for i in range(NY * NC)] for k in (3, 1, 2)]
X_SHIFTS = [[(i, i // NX * NX + (i + k) % NX) for i in range(NZ * NX)] for k in range(NX)]
GROUPS_Z = [[z * NX + x for z in range(NZ)] for x in range(NX)]
CORE_SWAP = [(i, i ^ 1) for i in range(NY * NC)]

T = 64
F = 2048
S = 1024
H = S // 2
N = NZ * NX
TB, FB = T // NZ, F // NX
TILES = (T // 8) * (H // 128)

f32, bf16 = jnp.float32, jnp.bfloat16
QUARTER = ((T // 8 * FB // 128, 8, 128), f32)
LINE = FB // 128
HALF = ((TILES + 1, 8, 128), f32)
TINY = 1e-35
VMEM = pl.BlockSpec(memory_space=pltpu.VMEM)
NN = (((1,), (0,)), ((), ()))
PIECES = 4
PIECE = S // PIECES


def call(kernel, outs, name, mib=10):
    shapes = [pltpu.VMEM(shape, dtype) for shape, dtype in outs]
    def run(*args):
        return pl.pallas_call(
            kernel,
            in_specs=[VMEM] * len(args),
            out_specs=[VMEM] * len(shapes),
            out_shape=shapes,
            compiler_params=pltpu.CompilerParams(vmem_limit_bytes=mib * 2**20),
            name=name,
        )(*args)
    return run


def split(value):
    high = value.astype(bf16)
    return high, (value - high.astype(f32)).astype(bf16)


def product(both, high, a_high, a_low):
    first = lax.dot_general(both, a_high, NN, preferred_element_type=f32)
    second = lax.dot_general(high, a_low, NN, preferred_element_type=f32)
    return first[:T] + first[T:] + second


def block_in(ref, z):
    return jnp.concatenate([ref[z * LINE + j] for j in range(LINE)], axis=1)


def half_in(ref):
    lines = [[ref[i * (H // 128) + j] for j in range(H // 128)] for i in range(T // 8)]
    return jnp.concatenate([jnp.concatenate(line, axis=1) for line in lines], axis=0)


def put_half(ref, value):
    for i in range(T // 8):
        for j in range(H // 128):
            ref[i * (H // 128) + j] = value[8 * i : 8 * i + 8, 128 * j : 128 * j + 128]


def wide(ref):
    rows = [jnp.concatenate([ref[z * NX + x] for x in range(NX)], axis=1) for z in range(NZ)]
    return jnp.concatenate(rows, axis=0)


def quarter(shift):
    at = (lax.axis_index("samp") + shift) % NX
    return at, pl.ds(pl.multiple_of(at * FB, FB), FB)


def row_of(value):
    total = value[:, :128]
    for at in range(128, value.shape[1], 128):
        total = total + value[:, at : at + 128]
    return jnp.sum(total.T, axis=0, keepdims=True)


def rows_tile(rows):
    tile = jnp.concatenate(rows + [jnp.zeros((8 - len(rows), T), f32)], axis=0)
    return jnp.concatenate([tile, jnp.zeros((8, 128 - T), f32)], axis=1)


def columns_of(tile, count):
    turned = tile.T
    return [turned[:T, i : i + 1] for i in range(count)]


def scale0(tile):
    (square,) = columns_of(tile, 1)
    return lax.rsqrt(jnp.maximum(square, TINY))


def scale1(tile):
    overlap, square = columns_of(tile, 2)
    left = jnp.maximum(square - overlap * overlap, 1e-6 * square)
    return overlap, lax.rsqrt(jnp.maximum(left, TINY))


def tile_in(own_ref):
    return own_ref[TILES]


def first_kernel(a_hbm, b_hbm, out_ref, both_ref, high_ref, low_ref, a_ref, b_ref, sems):
    copies = [pltpu.make_async_copy(b_hbm, b_ref, sems.at[PIECES])]
    for i in range(PIECES):
        rows = pl.ds(i * PIECE, PIECE)
        copies.append(pltpu.make_async_copy(a_hbm.at[rows, :], a_ref.at[i], sems.at[i]))
    for copy in copies:
        copy.start()
    copies[0].wait()
    high, low = split(b_ref[...])
    both = jnp.concatenate([high, low], axis=0)
    for i in range(PIECES):
        copies[i + 1].wait()
        a_high, a_low = split(a_ref[i])
        rows = slice(i * PIECE, (i + 1) * PIECE)
        high_ref[rows, :] = a_high
        low_ref[rows, :] = a_low
    both_ref[...] = both
    _, at = quarter(2)
    put_half(out_ref, product(both, high, high_ref[:, at], low_ref[:, at]))


def first_more_kernel(shift, both_ref, high_ref, low_ref, out_ref):
    both = both_ref[...]
    _, at = quarter(shift)
    put_half(out_ref, product(both, both[:T], high_ref[:, at], low_ref[:, at]))


def first_last_kernel(both_ref, high_ref, low_ref, out_ref, high_t_ref, low_t_ref):
    first_more_kernel(0, both_ref, high_ref, low_ref, out_ref)
    for rows in (slice(i, i + PIECE) for i in range(0, S, PIECE)):
        for columns in (slice(i, i + PIECE) for i in range(0, F, PIECE)):
            high_t_ref[columns, rows] = high_ref[rows, columns].T
            low_t_ref[columns, rows] = low_ref[rows, columns].T


def first(a, b_t):
    anywhere = pl.BlockSpec(memory_space=pltpu.HBM)
    a = pltpu.with_memory_space_constraint(a, pltpu.HBM)
    b_t = pltpu.with_memory_space_constraint(b_t, pltpu.HBM)
    return pl.pallas_call(
        first_kernel,
        in_specs=[anywhere, anywhere],
        out_specs=[VMEM] * 4,
        out_shape=[
            pltpu.VMEM(*QUARTER),
            pltpu.VMEM((2 * T, S), bf16),
            pltpu.VMEM((S, F), bf16),
            pltpu.VMEM((S, F), bf16),
        ],
        scratch_shapes=[
            pltpu.VMEM((PIECES, PIECE, F), f32),
            pltpu.VMEM((T, S), f32),
            pltpu.SemaphoreType.DMA((PIECES + 1,)),
        ],
        compiler_params=pltpu.CompilerParams(vmem_limit_bytes=16 * 2**20),
        name="first",
    )(a, b_t)


def add_kernel(*refs):
    total = refs[0][...]
    for ref in refs[1:-1]:
        total = total + ref[...]
    refs[-1][...] = total


def lines_kernel(*refs):
    out_ref = refs[-1]
    for z in range(NZ):
        for j in range(out_ref.shape[1]):
            at = z * LINE + j if j < LINE else NZ * LINE
            total = refs[0][at]
            for ref in refs[1:-1]:
                total = total + ref[at]
            out_ref[z, j] = total


def sum_lines_kernel(in_ref, out_ref, *tile_refs):
    total = in_ref[0]
    for z in range(1, NZ):
        total = total + in_ref[z]
    block = jnp.concatenate([total[j] for j in range(LINE)], axis=1)
    for i in range(N):
        out_ref[i] = block
    for tile_ref in tile_refs:
        tile_ref[...] = total[LINE]


def sum_over_samp(parts):
    tiles = parts[0].shape[0] - NZ * LINE
    got = [lax.ppermute(parts[k], "samp", X_SHIFTS[k]) for k in (3, 1, 2)]
    (part,) = call(lines_kernel, [((NZ, LINE + tiles, 8, 128), f32)], "sum_x")(parts[0], *got)
    got = lax.all_to_all(part, "samp", 0, 0, axis_index_groups=GROUPS_Z)
    outs = [((N, TB, FB), f32)] + [((8, 128), f32)] * tiles
    part, *tile = call(sum_lines_kernel, outs, "sum_z")(got)
    return lax.all_to_all(part, "samp", 0, 0), *tile


def half_rows(own):
    core = lax.axis_index("feat") % NC
    at = core if own else 1 - core
    return pl.ds(pl.multiple_of(at * H, H), H)


def forward_send(value, scalars, high_ref, low_ref, send_ref, both_ref):
    high, low = split(value)
    both = jnp.concatenate([high, low], axis=0)
    both_ref[...] = both
    at = half_rows(False)
    put_half(send_ref, product(both, high, high_ref[:, at], low_ref[:, at]))
    send_ref[TILES] = rows_tile(scalars)


def send0_kernel(g_ref, high_ref, low_ref, send_ref, both_ref):
    g = wide(g_ref)
    forward_send(g, [row_of(g * g)], high_ref, low_ref, send_ref, both_ref)


def send1_kernel(g_ref, own0_ref, w_ref, high_ref, low_ref, send_ref, both_ref):
    e0 = wide(g_ref) * scale0(tile_in(own0_ref))
    w = wide(w_ref)
    forward_send(w, [row_of(e0 * w), row_of(w * w)], high_ref, low_ref, send_ref, both_ref)


def basis01(g_ref, own0_ref, w1_ref, own1_ref):
    e0 = wide(g_ref) * scale0(tile_in(own0_ref))
    overlap, scale = scale1(tile_in(own1_ref))
    return e0, (wide(w1_ref) - overlap * e0) * scale


def send2_kernel(
    g_ref, own0_ref, w1_ref, own1_ref, w_ref, tile_ref, high_ref, low_ref, send_ref, both_ref, q_ref
):
    e0, e1 = basis01(g_ref, own0_ref, w1_ref, own1_ref)
    overlap0, overlap1 = columns_of(tile_ref[...], 2)
    q = wide(w_ref) - overlap0 * e0 - overlap1 * e1
    q_ref[...] = q
    pairs = [(e0, e0), (e0, e1), (e0, q), (e1, e1), (e1, q), (q, q)]
    scalars = [row_of(p * q) for p, q in pairs]
    forward_send(q, scalars, high_ref, low_ref, send_ref, both_ref)


def keep_kernel(both_ref, send_ref, high_ref, low_ref, keep_ref):
    both = both_ref[...]
    at = half_rows(True)
    put_half(keep_ref, product(both, both[:T], high_ref[:, at], low_ref[:, at]))
    keep_ref[TILES] = send_ref[TILES]


def sum_over_feat(kernel, args, turned, name, extra=()):
    outs = [HALF, ((2 * T, F), bf16), *extra]
    send, both, *extra = call(kernel, outs, name)(*args, *turned)
    got = lax.ppermute(send, "feat", CORE_SWAP)
    (keep,) = call(keep_kernel, [HALF], "keep")(both, send, *turned)
    (part,) = call(add_kernel, [HALF], "add")(keep, got)
    got = [lax.ppermute(part, "feat", shift) for shift in Y_SHIFTS]
    (own,) = call(add_kernel, [HALF], "sum_y")(part, *got)
    return own, lax.ppermute(own, "feat", CORE_SWAP), *extra


def image0(tile_ref, half0_ref):
    return half_in(half0_ref) * scale0(tile_in(tile_ref))


def image1(tile0_ref, half0_ref, tile1_ref, half1_ref):
    overlap, scale = scale1(tile_in(tile1_ref))
    return (half_in(half1_ref) - overlap * image0(tile0_ref, half0_ref)) * scale


def back_own(value, high_ref, low_ref, out_ref):
    high, low = split(value)
    both = jnp.concatenate([high, low], axis=0)
    rows = half_rows(True)
    for x in range(NX):
        at = slice(x * FB, (x + 1) * FB)
        out_ref[x] = product(both, high, high_ref[rows, at], low_ref[rows, at])


def ready(value, both_ref):
    high, low = split(value)
    both_ref[...] = jnp.concatenate([high, low], axis=0)


def back_other_kernel(shift, both_ref, acc_ref, high_ref, low_ref, *refs):
    both = both_ref[...]
    rows = half_rows(False)
    place, at = quarter(shift)
    out_ref = refs[-1]
    put_half(out_ref, acc_ref[place] + product(both, both[:T], high_ref[rows, at], low_ref[rows, at]))
    for tile_ref in refs[:-1]:
        out_ref[NZ * LINE] = tile_ref[...]


def back0_own_kernel(own0_ref, high_ref, low_ref, out_ref):
    back_own(image0(own0_ref, own0_ref), high_ref, low_ref, out_ref)


def back0_ready_kernel(own0_ref, other0_ref, both_ref):
    ready(image0(own0_ref, other0_ref), both_ref)


def overlaps(u0, u1):
    return rows_tile([row_of(u0 * u1), row_of(u1 * u1)])


def back1_own_kernel(own0_ref, own1_ref, high_ref, low_ref, out_ref, tile_ref):
    u1 = image1(own0_ref, own0_ref, own1_ref, own1_ref)
    back_own(u1, high_ref, low_ref, out_ref)
    tile_ref[...] = overlaps(image0(own0_ref, own0_ref), u1)


def back1_ready_kernel(own0_ref, other0_ref, own1_ref, other1_ref, tile_ref, both_ref, out_tile_ref):
    u1 = image1(own0_ref, other0_ref, own1_ref, other1_ref)
    ready(u1, both_ref)
    out_tile_ref[...] = tile_ref[...] + overlaps(image0(own0_ref, other0_ref), u1)


def transposed(own_kernel, ready_kernel, owns, halves, a_high, a_low, tiles, name):
    tile = [((8, 128), f32)] * tiles
    outs = [((NX, T, FB), f32)] + tile
    acc, *scalars = call(own_kernel, outs, name + "_own")(*owns, a_high, a_low)
    outs = [((2 * T, H), bf16)] + tile
    both, *scalars = call(ready_kernel, outs, name + "_ready")(*halves, *scalars)
    parts = [None] * NX
    (count, *rest), dtype = QUARTER
    for k in (2, 1, 3, 0):
        kernel = functools.partial(back_other_kernel, k)
        outs = [((count + tiles, *rest), dtype)]
        (parts[k],) = call(kernel, outs, name + "_other")(both, acc, a_high, a_low, *scalars)
    return parts


PAIRS = [(0, 0), (0, 1), (0, 2), (1, 1), (1, 2), (2, 2)]


def images(own0_ref, own1_ref, own2_ref, half0_ref, half1_ref, half2_ref):
    u0 = image0(own0_ref, half0_ref)
    u1 = image1(own0_ref, half0_ref, own1_ref, half1_ref)
    square = columns_of(tile_in(own2_ref), 6)[5]
    return u0, u1, half_in(half2_ref) * lax.rsqrt(jnp.maximum(square, TINY))


def gram_rows(*refs):
    u = images(*refs)
    return rows_tile([row_of(u[i] * u[j]) for i, j in PAIRS])


def gram_own_kernel(own0_ref, own1_ref, own2_ref, out_ref):
    out_ref[...] = gram_rows(own0_ref, own1_ref, own2_ref, own0_ref, own1_ref, own2_ref)


def gram_kernel(own0_ref, other0_ref, own1_ref, other1_ref, own2_ref, other2_ref, tile_ref, out_ref):
    tile = tile_ref[...]
    tile += gram_rows(own0_ref, own1_ref, own2_ref, other0_ref, other1_ref, other2_ref)
    for i in range(out_ref.shape[0]):
        out_ref[i] = tile


def solve(gram, dots, square0, ridge):
    scale2 = lax.rsqrt(jnp.maximum(dots[5], TINY))
    e = [dots[0], dots[1], dots[2] * scale2, dots[3], dots[4] * scale2, dots[5] * scale2 * scale2]
    k00, k01, k02, k11, k12, k22 = [u + ridge * v for u, v in zip(gram, e)]
    norm = jnp.sqrt(square0)
    r0, r1, r2 = e[0] * norm, e[1] * norm, e[2] * norm
    inverse0 = 1.0 / jnp.maximum(k00, TINY)
    l10, l20 = k01 * inverse0, k02 * inverse0
    d1 = k11 - l10 * k01
    inverse1 = jnp.where(d1 > 1e-6 * k11, 1.0 / jnp.maximum(d1, TINY), 0.0)
    t = k12 - l20 * k01
    l21 = t * inverse1
    d2 = k22 - l20 * k02 - l21 * t
    inverse2 = jnp.where(d2 > 1e-6 * k22, 1.0 / jnp.maximum(d2, TINY), 0.0)
    z1 = r1 - l10 * r0
    z2 = r2 - l20 * r0 - l21 * z1
    c2 = z2 * inverse2
    c1 = z1 * inverse1 - l21 * c2
    c0 = r0 * inverse0 - l10 * c1 - l20 * c2
    return c0, c1, c2, c2 * scale2


def last_kernel(
    gram_ref, ridge_ref, b_ref, g_ref, w1_ref, q_ref,
    own0_ref, other0_ref, own1_ref, other1_ref, own2_ref, other2_ref, x_ref, r_ref,
):
    gram = gram_ref[0]
    for i in range(1, gram_ref.shape[0]):
        gram = gram + gram_ref[i]
    dots = tile_in(own2_ref)
    row = lambda tile, i: tile[i : i + 1, :]
    coefficients = solve(
        [row(gram, i) for i in range(6)],
        [row(dots, i) for i in range(6)],
        row(tile_in(own0_ref), 0),
        jnp.concatenate([ridge_ref[...], jnp.zeros((1, 128 - T), f32)], axis=1),
    )
    tile = jnp.concatenate(list(coefficients) + [jnp.zeros((4, 128), f32)], axis=0)
    c0, c1, _, c2 = columns_of(tile, 4)
    e0, e1 = basis01(g_ref, own0_ref, w1_ref, own1_ref)
    x_ref[...] = c0 * e0 + c1 * e1 + c2 * q_ref[...]
    for own, half0_ref, half1_ref, half2_ref in (
        (True, own0_ref, own1_ref, own2_ref),
        (False, other0_ref, other1_ref, other2_ref),
    ):
        u0 = image0(own0_ref, half0_ref)
        u1 = image1(own0_ref, half0_ref, own1_ref, half1_ref)
        at = half_rows(own)
        r_ref[:, at] = b_ref[:, at] - c0 * u0 - c1 * u1 - c2 * half_in(half2_ref)


def last(*args):
    return pl.pallas_call(
        last_kernel,
        in_specs=[VMEM] * len(args),
        out_specs=[VMEM, VMEM],
        out_shape=[jax.ShapeDtypeStruct((T, F), f32), jax.ShapeDtypeStruct((T, S), f32)],
        compiler_params=pltpu.CompilerParams(vmem_limit_bytes=16 * 2**20),
        name="last",
    )(*args)


def per_device(features, targets, ridge):
    b_t = targets.T
    parts = {}
    parts[2], both, a_high, a_low = first(features, b_t)
    for k in (1, 3):
        kernel = functools.partial(first_more_kernel, k)
        (parts[k],) = call(kernel, [QUARTER], "first_more")(both, a_high, a_low)
    outs = [QUARTER, ((F, S), bf16), ((F, S), bf16)]
    parts[0], *turned = call(first_last_kernel, outs, "first_last")(both, a_high, a_low)
    (g,) = sum_over_samp(parts)
    own0, other0 = sum_over_feat(send0_kernel, (g,), turned, "send0")
    parts = transposed(
        back0_own_kernel, back0_ready_kernel, (own0,), (own0, other0), a_high, a_low, 0, "back0"
    )
    (w1,) = sum_over_samp(parts)
    own1, other1 = sum_over_feat(send1_kernel, (g, own0, w1), turned, "send1")
    halves = (own0, other0, own1, other1)
    parts = transposed(
        back1_own_kernel, back1_ready_kernel, (own0, own1), halves, a_high, a_low, 1, "back1"
    )
    w2, tile = sum_over_samp(parts)
    args = (g, own0, w1, own1, w2, tile)
    own2, other2, q = sum_over_feat(send2_kernel, args, turned, "send2", [((T, F), f32)])
    halves = (own0, other0, own1, other1, own2, other2)
    (tile,) = call(gram_own_kernel, [((8, 128), f32)], "gram_own")(own0, own1, own2)
    (tiles,) = call(gram_kernel, [((N, 8, 128), f32)], "gram")(*halves, tile)
    gram = lax.all_to_all(tiles, "samp", 0, 0)
    x, r = last(gram, ridge.reshape(1, T), b_t, g, w1, q, *halves)
    return x.T, r.T


def solution(mesh):
    placed = (P("samp", "feat"), P("samp", None), P())
    return jax.shard_map(
        per_device,
        mesh=mesh,
        in_specs=placed,
        out_specs=(P("feat", None), P("samp", None)),
        check_vma=False,
    )
```

```python
import functools

import jax
import jax.numpy as jnp
from jax import lax
from jax.experimental import pallas as pl
from jax.experimental.pallas import tpu as pltpu
from jax.sharding import PartitionSpec as P

NZ, NX, NY, NC = 8, 4, 4, 2
Y_SHIFTS = [[(i, (i + NC * k) % (NY * NC)) for i in range(NY * NC)] for k in (3, 1, 2)]
X_SHIFTS = [[(i, i // NX * NX + (i + k) % NX) for i in range(NZ * NX)] for k in range(NX)]
GROUPS_Z = [[z * NX + x for z in range(NZ)] for x in range(NX)]
SENT = (2, 1, 3)
CORE_SWAP = [(i, i ^ 1) for i in range(NY * NC)]

T = 64
F = 2048
S = 1024
H = S // 2
N = NZ * NX
TB, FB = T // NZ, F // NX
TILES = (T // 8) * (H // 128)

f32, bf16 = jnp.float32, jnp.bfloat16
QUARTER = ((T // 8 * FB // 128, 8, 128), f32)
LINE = FB // 128
HALF = ((TILES + 1, 8, 128), f32)
TINY = 1e-35
VMEM = pl.BlockSpec(memory_space=pltpu.VMEM)
NN = (((1,), (0,)), ((), ()))
PIECES = 4
PIECE = S // PIECES


def call(kernel, outs, name, mib=10):
    shapes = [pltpu.VMEM(shape, dtype) for shape, dtype in outs]
    def run(*args):
        return pl.pallas_call(
            kernel,
            in_specs=[VMEM] * len(args),
            out_specs=[VMEM] * len(shapes),
            out_shape=shapes,
            compiler_params=pltpu.CompilerParams(vmem_limit_bytes=mib * 2**20),
            name=name,
        )(*args)
    return run


def split(value):
    high = value.astype(bf16)
    return high, (value - high.astype(f32)).astype(bf16)


def product(both, high, a_high, a_low):
    first = lax.dot_general(both, a_high, NN, preferred_element_type=f32)
    second = lax.dot_general(high, a_low, NN, preferred_element_type=f32)
    return first[:T] + first[T:] + second


def block_in(ref, z):
    return jnp.concatenate([ref[z * LINE + j] for j in range(LINE)], axis=1)


def half_in(ref):
    lines = [[ref[i * (H // 128) + j] for j in range(H // 128)] for i in range(T // 8)]
    return jnp.concatenate([jnp.concatenate(line, axis=1) for line in lines], axis=0)


def put_half(ref, value):
    for i in range(T // 8):
        for j in range(H // 128):
            ref[i * (H // 128) + j] = value[8 * i : 8 * i + 8, 128 * j : 128 * j + 128]


def wide(ref):
    rows = [jnp.concatenate([ref[z * NX + x] for x in range(NX)], axis=1) for z in range(NZ)]
    return jnp.concatenate(rows, axis=0)


def quarter(shift):
    at = (lax.axis_index("samp") + shift) % NX
    return at, pl.ds(pl.multiple_of(at * FB, FB), FB)


def row_of(value):
    total = value[:, :128]
    for at in range(128, value.shape[1], 128):
        total = total + value[:, at : at + 128]
    return jnp.sum(total.T, axis=0, keepdims=True)


def rows_tile(rows):
    tile = jnp.concatenate(rows + [jnp.zeros((8 - len(rows), T), f32)], axis=0)
    return jnp.concatenate([tile, jnp.zeros((8, 128 - T), f32)], axis=1)


def columns_of(tile, count):
    turned = tile.T
    return [turned[:T, i : i + 1] for i in range(count)]


def scale0(tile):
    (square,) = columns_of(tile, 1)
    return lax.rsqrt(jnp.maximum(square, TINY))


def scale1(tile):
    overlap, square = columns_of(tile, 2)
    left = jnp.maximum(square - overlap * overlap, 1e-6 * square)
    return overlap, lax.rsqrt(jnp.maximum(left, TINY))


def tile_in(own_ref):
    return own_ref[TILES]


def first_kernel(a_hbm, b_hbm, out_ref, both_ref, high_ref, low_ref, a_ref, b_ref, sems):
    copies = [pltpu.make_async_copy(b_hbm, b_ref, sems.at[PIECES])]
    for i in range(PIECES):
        rows = pl.ds(i * PIECE, PIECE)
        copies.append(pltpu.make_async_copy(a_hbm.at[rows, :], a_ref.at[i], sems.at[i]))
    for copy in copies:
        copy.start()
    copies[0].wait()
    high, low = split(b_ref[...])
    both = jnp.concatenate([high, low], axis=0)
    for i in range(PIECES):
        copies[i + 1].wait()
        a_high, a_low = split(a_ref[i])
        rows = slice(i * PIECE, (i + 1) * PIECE)
        high_ref[rows, :] = a_high
        low_ref[rows, :] = a_low
    both_ref[...] = both
    _, at = quarter(2)
    put_half(out_ref, product(both, high, high_ref[:, at], low_ref[:, at]))


def first_more_kernel(shift, both_ref, high_ref, low_ref, out_ref):
    both = both_ref[...]
    _, at = quarter(shift)
    put_half(out_ref, product(both, both[:T], high_ref[:, at], low_ref[:, at]))


def first_last_kernel(both_ref, high_ref, low_ref, out_ref, high_t_ref, low_t_ref):
    first_more_kernel(0, both_ref, high_ref, low_ref, out_ref)
    for rows in (slice(i, i + PIECE) for i in range(0, S, PIECE)):
        for columns in (slice(i, i + PIECE) for i in range(0, F, PIECE)):
            high_t_ref[columns, rows] = high_ref[rows, columns].T
            low_t_ref[columns, rows] = low_ref[rows, columns].T


def first(a, b_t):
    anywhere = pl.BlockSpec(memory_space=pltpu.HBM)
    a = pltpu.with_memory_space_constraint(a, pltpu.HBM)
    b_t = pltpu.with_memory_space_constraint(b_t, pltpu.HBM)
    return pl.pallas_call(
        first_kernel,
        in_specs=[anywhere, anywhere],
        out_specs=[VMEM] * 4,
        out_shape=[
            pltpu.VMEM(*QUARTER),
            pltpu.VMEM((2 * T, S), bf16),
            pltpu.VMEM((S, F), bf16),
            pltpu.VMEM((S, F), bf16),
        ],
        scratch_shapes=[
            pltpu.VMEM((PIECES, PIECE, F), f32),
            pltpu.VMEM((T, S), f32),
            pltpu.SemaphoreType.DMA((PIECES + 1,)),
        ],
        compiler_params=pltpu.CompilerParams(vmem_limit_bytes=16 * 2**20),
        name="first",
    )(a, b_t)


def add_kernel(*refs):
    total = refs[0][...]
    for ref in refs[1:-1]:
        total = total + ref[...]
    refs[-1][...] = total


def lines_kernel(*refs):
    out_ref = refs[-1]
    for z in range(NZ):
        for j in range(out_ref.shape[1]):
            at = z * LINE + j if j < LINE else NZ * LINE
            total = refs[0][at]
            for ref in refs[1:-1]:
                total = total + ref[at]
            out_ref[z, j] = total


def sum_lines_kernel(in_ref, out_ref, *tile_refs):
    total = in_ref[0]
    for z in range(1, NZ):
        total = total + in_ref[z]
    block = jnp.concatenate([total[j] for j in range(LINE)], axis=1)
    for i in range(N):
        out_ref[i] = block
    for tile_ref in tile_refs:
        tile_ref[...] = total[LINE]


def sum_over_samp(parts):
    tiles = parts[0].shape[0] - NZ * LINE
    got = [lax.ppermute(parts[k], "samp", X_SHIFTS[k]) for k in (3, 1, 2)]
    (part,) = call(lines_kernel, [((NZ, LINE + tiles, 8, 128), f32)], "sum_x")(parts[0], *got)
    got = lax.all_to_all(part, "samp", 0, 0, axis_index_groups=GROUPS_Z)
    outs = [((N, TB, FB), f32)] + [((8, 128), f32)] * tiles
    part, *tile = call(sum_lines_kernel, outs, "sum_z")(got)
    return lax.all_to_all(part, "samp", 0, 0), *tile


def half_rows(own):
    core = lax.axis_index("feat") % NC
    at = core if own else 1 - core
    return pl.ds(pl.multiple_of(at * H, H), H)


def forward_send(value, scalars, high_ref, low_ref, send_ref, both_ref):
    high, low = split(value)
    both = jnp.concatenate([high, low], axis=0)
    both_ref[...] = both
    at = half_rows(False)
    put_half(send_ref, product(both, high, high_ref[:, at], low_ref[:, at]))
    send_ref[TILES] = rows_tile(scalars)


def send0_kernel(g_ref, high_ref, low_ref, send_ref, both_ref):
    g = wide(g_ref)
    forward_send(g, [row_of(g * g)], high_ref, low_ref, send_ref, both_ref)


def send1_kernel(g_ref, own0_ref, w_ref, high_ref, low_ref, send_ref, both_ref):
    e0 = wide(g_ref) * scale0(tile_in(own0_ref))
    w = wide(w_ref)
    forward_send(w, [row_of(e0 * w), row_of(w * w)], high_ref, low_ref, send_ref, both_ref)


def basis01(g_ref, own0_ref, w1_ref, own1_ref):
    e0 = wide(g_ref) * scale0(tile_in(own0_ref))
    overlap, scale = scale1(tile_in(own1_ref))
    return e0, (wide(w1_ref) - overlap * e0) * scale


def send2_kernel(
    g_ref, own0_ref, w1_ref, own1_ref, w_ref, tile_ref, high_ref, low_ref, send_ref, both_ref, q_ref
):
    e0, e1 = basis01(g_ref, own0_ref, w1_ref, own1_ref)
    overlap0, overlap1 = columns_of(tile_ref[...], 2)
    q = (wide(w_ref) - overlap0 * e0 - overlap1 * e1) * (1.0 / jnp.maximum(overlap1, TINY))
    q_ref[...] = q
    forward_send(q, [jnp.zeros((1, T), f32)], high_ref, low_ref, send_ref, both_ref)


def keep2_kernel(both_ref, g_ref, own0_ref, w1_ref, own1_ref, q_ref, high_ref, low_ref, keep_ref):
    both = both_ref[...]
    at = half_rows(True)
    put_half(keep_ref, product(both, both[:T], high_ref[:, at], low_ref[:, at]))
    e0, e1 = basis01(g_ref, own0_ref, w1_ref, own1_ref)
    q = q_ref[...]
    pairs = [(e0, e0), (e0, e1), (e0, q), (e1, e1), (e1, q), (q, q)]
    keep_ref[TILES] = rows_tile([row_of(left * right) for left, right in pairs])


def keep_kernel(both_ref, send_ref, high_ref, low_ref, keep_ref):
    both = both_ref[...]
    at = half_rows(True)
    put_half(keep_ref, product(both, both[:T], high_ref[:, at], low_ref[:, at]))
    keep_ref[TILES] = send_ref[TILES]


def sum_over_feat(kernel, args, turned, name):
    outs = [HALF, ((2 * T, F), bf16)]
    send, both = call(kernel, outs, name)(*args, *turned)
    got = lax.ppermute(send, "feat", CORE_SWAP)
    (keep,) = call(keep_kernel, [HALF], "keep")(both, send, *turned)
    return add_over_feat(keep, got)


def add_over_feat(keep, got):
    (part,) = call(add_kernel, [HALF], "add")(keep, got)
    got = [lax.ppermute(part, "feat", shift) for shift in Y_SHIFTS]
    (own,) = call(add_kernel, [HALF], "sum_y")(part, *got)
    return own, lax.ppermute(own, "feat", CORE_SWAP)


def image0(tile_ref, half0_ref):
    return half_in(half0_ref) * scale0(tile_in(tile_ref))


def image1(tile0_ref, half0_ref, tile1_ref, half1_ref):
    overlap, scale = scale1(tile_in(tile1_ref))
    return (half_in(half1_ref) - overlap * image0(tile0_ref, half0_ref)) * scale


def back_own(value, high_ref, low_ref, out_ref):
    high, low = split(value)
    both = jnp.concatenate([high, low], axis=0)
    rows = half_rows(True)
    for x in range(NX):
        at = slice(x * FB, (x + 1) * FB)
        out_ref[x] = product(both, high, high_ref[rows, at], low_ref[rows, at])


def back_quarter(shift, both, acc_ref, high_ref, low_ref, out_ref, *tiles):
    rows = half_rows(False)
    place, at = quarter(shift)
    put_half(out_ref, acc_ref[place] + product(both, both[:T], high_ref[rows, at], low_ref[rows, at]))
    for tile in tiles:
        out_ref[NZ * LINE] = tile


def back_others(value, acc_ref, high_ref, low_ref, out_refs, both_ref, *tiles):
    high, low = split(value)
    both = jnp.concatenate([high, low], axis=0)
    both_ref[...] = both
    for shift, out_ref in zip(SENT, out_refs):
        back_quarter(shift, both, acc_ref, high_ref, low_ref, out_ref, *tiles)


def back_mine_kernel(both_ref, acc_ref, high_ref, low_ref, *refs):
    tiles = [ref[...] for ref in refs[:-1]]
    back_quarter(0, both_ref[...], acc_ref, high_ref, low_ref, refs[-1], *tiles)


def back0_own_kernel(own0_ref, high_ref, low_ref, out_ref):
    back_own(image0(own0_ref, own0_ref), high_ref, low_ref, out_ref)


def back0_others_kernel(own0_ref, other0_ref, acc_ref, high_ref, low_ref, *refs):
    value = image0(own0_ref, other0_ref)
    back_others(value, acc_ref, high_ref, low_ref, refs[:-1], refs[-1])


def overlaps(u0, u1):
    return rows_tile([row_of(u0 * u1), row_of(u1 * u1)])


def back1_own_kernel(own0_ref, own1_ref, high_ref, low_ref, out_ref, tile_ref):
    u1 = image1(own0_ref, own0_ref, own1_ref, own1_ref)
    back_own(u1, high_ref, low_ref, out_ref)
    tile_ref[...] = overlaps(image0(own0_ref, own0_ref), u1)


def back1_others_kernel(
    own0_ref, other0_ref, own1_ref, other1_ref, tile_ref, acc_ref, high_ref, low_ref, *refs
):
    value = image1(own0_ref, other0_ref, own1_ref, other1_ref)
    tile = tile_ref[...] + overlaps(image0(own0_ref, other0_ref), value)
    refs[-1][...] = tile
    back_others(value, acc_ref, high_ref, low_ref, refs[:-2], refs[-2], tile)


def transposed(own_kernel, others_kernel, owns, halves, a_high, a_low, tiles, name):
    tile = [((8, 128), f32)] * tiles
    outs = [((NX, T, FB), f32)] + tile
    acc, *scalars = call(own_kernel, outs, name + "_own")(*owns, a_high, a_low)
    (count, *rest), dtype = QUARTER
    part = ((count + tiles, *rest), dtype)
    outs = [part] * len(SENT) + [((2 * T, H), bf16)] + tile
    args = (*halves, *scalars, acc, a_high, a_low)
    results = call(others_kernel, outs, name + "_others")(*args)
    sent, (both, *scalars) = results[: len(SENT)], results[len(SENT) :]
    (mine,) = call(back_mine_kernel, [part], name + "_mine")(both, acc, a_high, a_low, *scalars)
    return {0: mine, **dict(zip(SENT, sent))}


PAIRS = [(0, 0), (0, 1), (0, 2), (1, 1), (1, 2), (2, 2)]


def gram_rows(own, u_ref, half2_ref):
    at = half_rows(own)
    u = u_ref[0, :, at], u_ref[1, :, at], half_in(half2_ref)
    return rows_tile([row_of(u[i] * u[j]) for i, j in PAIRS])


def gram_own_kernel(u_ref, own2_ref, out_ref):
    out_ref[...] = gram_rows(True, u_ref, own2_ref)


def gram_kernel(u_ref, other2_ref, tile_ref, out_ref):
    tile = tile_ref[...] + gram_rows(False, u_ref, other2_ref)
    for i in range(out_ref.shape[0]):
        out_ref[i] = tile


def solve(gram, dots, square0, ridge):
    k00, k01, k02, k11, k12, k22 = [u + ridge * v for u, v in zip(gram, dots)]
    norm = jnp.sqrt(square0)
    r0, r1, r2 = dots[0] * norm, dots[1] * norm, dots[2] * norm
    inverse0 = 1.0 / jnp.maximum(k00, TINY)
    l10, l20 = k01 * inverse0, k02 * inverse0
    d1 = k11 - l10 * k01
    inverse1 = jnp.where(d1 > 1e-6 * k11, 1.0 / jnp.maximum(d1, TINY), 0.0)
    t = k12 - l20 * k01
    l21 = t * inverse1
    d2 = k22 - l20 * k02 - l21 * t
    inverse2 = jnp.where(d2 > 1e-6 * k22, 1.0 / jnp.maximum(d2, TINY), 0.0)
    z1 = r1 - l10 * r0
    z2 = r2 - l20 * r0 - l21 * z1
    c2 = z2 * inverse2
    c1 = z1 * inverse1 - l21 * c2
    c0 = r0 * inverse0 - l10 * c1 - l20 * c2
    return c0, c1, c2


def basis_kernel(g_ref, own0_ref, w1_ref, own1_ref, other0_ref, other1_ref, e_ref, u_ref):
    e_ref[0], e_ref[1] = basis01(g_ref, own0_ref, w1_ref, own1_ref)
    for own, half0_ref, half1_ref in ((True, own0_ref, own1_ref), (False, other0_ref, other1_ref)):
        at = half_rows(own)
        u_ref[0, :, at] = image0(own0_ref, half0_ref)
        u_ref[1, :, at] = image1(own0_ref, half0_ref, own1_ref, half1_ref)


def last_kernel(
    gram_ref, ridge_ref, b_ref, e_ref, q_ref, u_ref, own0_ref, own2_ref, other2_ref, x_ref, r_ref
):
    gram = gram_ref[0]
    for i in range(1, gram_ref.shape[0]):
        gram = gram + gram_ref[i]
    dots = tile_in(own2_ref) + tile_in(other2_ref)
    row = lambda tile, i: tile[i : i + 1, :]
    coefficients = solve(
        [row(gram, i) for i in range(6)],
        [row(dots, i) for i in range(6)],
        row(tile_in(own0_ref), 0),
        jnp.concatenate([ridge_ref[...], jnp.zeros((1, 128 - T), f32)], axis=1),
    )
    tile = jnp.concatenate(list(coefficients) + [jnp.zeros((5, 128), f32)], axis=0)
    c0, c1, c2 = columns_of(tile, 3)
    x_ref[...] = c0 * e_ref[0] + c1 * e_ref[1] + c2 * q_ref[...]
    for own, half2_ref in ((True, own2_ref), (False, other2_ref)):
        at = half_rows(own)
        r_ref[:, at] = b_ref[:, at] - c0 * u_ref[0, :, at] - c1 * u_ref[1, :, at] - c2 * half_in(half2_ref)


def last(*args):
    return pl.pallas_call(
        last_kernel,
        in_specs=[VMEM] * len(args),
        out_specs=[VMEM, VMEM],
        out_shape=[jax.ShapeDtypeStruct((T, F), f32), jax.ShapeDtypeStruct((T, S), f32)],
        compiler_params=pltpu.CompilerParams(vmem_limit_bytes=16 * 2**20),
        name="last",
    )(*args)


def per_device(features, targets, ridge):
    b_t = targets.T
    parts = {}
    parts[2], both, a_high, a_low = first(features, b_t)
    for k in (1, 3):
        kernel = functools.partial(first_more_kernel, k)
        (parts[k],) = call(kernel, [QUARTER], "first_more")(both, a_high, a_low)
    outs = [QUARTER, ((F, S), bf16), ((F, S), bf16)]
    parts[0], *turned = call(first_last_kernel, outs, "first_last")(both, a_high, a_low)
    (g,) = sum_over_samp(parts)
    own0, other0 = sum_over_feat(send0_kernel, (g,), turned, "send0")
    parts = transposed(
        back0_own_kernel, back0_others_kernel, (own0,), (own0, other0), a_high, a_low, 0, "back0"
    )
    (w1,) = sum_over_samp(parts)
    own1, other1 = sum_over_feat(send1_kernel, (g, own0, w1), turned, "send1")
    halves = (own0, other0, own1, other1)
    parts = transposed(
        back1_own_kernel, back1_others_kernel, (own0, own1), halves, a_high, a_low, 1, "back1"
    )
    w2, tile = sum_over_samp(parts)
    basis = (g, own0, w1, own1)
    outs = [HALF, ((2 * T, F), bf16), ((T, F), f32)]
    send, both, q = call(send2_kernel, outs, "send2")(*basis, w2, tile, *turned)
    got = lax.ppermute(send, "feat", CORE_SWAP)
    (keep,) = call(keep2_kernel, [HALF], "keep2")(both, *basis, q, *turned)
    own2, other2 = add_over_feat(keep, got)
    outs = [((2, T, F), f32), ((2, T, S), f32)]
    e, u = call(basis_kernel, outs, "basis")(*basis, other0, other1)
    (tile,) = call(gram_own_kernel, [((8, 128), f32)], "gram_own")(u, own2)
    (tiles,) = call(gram_kernel, [((N, 8, 128), f32)], "gram")(u, other2, tile)
    gram = lax.all_to_all(tiles, "samp", 0, 0)
    x, r = last(gram, ridge.reshape(1, T), b_t, e, q, u, own0, own2, other2)
    return x.T, r.T


def solution(mesh):
    placed = (P("samp", "feat"), P("samp", None), P())
    return jax.shard_map(
        per_device,
        mesh=mesh,
        in_specs=placed,
        out_specs=(P("feat", None), P("samp", None)),
        check_vma=False,
    )
```

```python
import functools

import jax
import jax.numpy as jnp
from jax import lax
from jax.experimental import pallas as pl
from jax.experimental.pallas import tpu as pltpu
from jax.sharding import PartitionSpec as P

NZ, NX, NY, NC = 8, 4, 4, 2
Y_SHIFTS = [[(i, (i + NC * k) % (NY * NC)) for i in range(NY * NC)] for k in (3, 1, 2)]
X_SHIFTS = [[(i, i // NX * NX + (i + k) % NX) for i in range(NZ * NX)] for k in range(NX)]
GROUPS_Z = [[z * NX + x for z in range(NZ)] for x in range(NX)]
SENT = (2, 1, 3)
CORE_SWAP = [(i, i ^ 1) for i in range(NY * NC)]

T = 64
F = 2048
S = 1024
H = S // 2
N = NZ * NX
TB, FB = T // NZ, F // NX
TILES = (T // 8) * (H // 128)

f32, bf16 = jnp.float32, jnp.bfloat16
QUARTER = ((T // 8 * FB // 128, 8, 128), f32)
LINE = FB // 128
HALF = ((TILES + 1, 8, 128), f32)
TINY = 1e-35
VMEM = pl.BlockSpec(memory_space=pltpu.VMEM)
NN = (((1,), (0,)), ((), ()))
PIECES = 4
PIECE = S // PIECES


def call(kernel, outs, name, mib=10):
    shapes = [pltpu.VMEM(shape, dtype) for shape, dtype in outs]
    def run(*args):
        return pl.pallas_call(
            kernel,
            in_specs=[VMEM] * len(args),
            out_specs=[VMEM] * len(shapes),
            out_shape=shapes,
            compiler_params=pltpu.CompilerParams(vmem_limit_bytes=mib * 2**20),
            name=name,
        )(*args)
    return run


def split(value):
    high = value.astype(bf16)
    return high, (value - high.astype(f32)).astype(bf16)


def product(both, high, a_high, a_low):
    first = lax.dot_general(both, a_high, NN, preferred_element_type=f32)
    second = lax.dot_general(high, a_low, NN, preferred_element_type=f32)
    return first[:T] + first[T:] + second


def block_in(ref, z):
    return jnp.concatenate([ref[z * LINE + j] for j in range(LINE)], axis=1)


def half_in(ref):
    lines = [[ref[i * (H // 128) + j] for j in range(H // 128)] for i in range(T // 8)]
    return jnp.concatenate([jnp.concatenate(line, axis=1) for line in lines], axis=0)


def put_half(ref, value):
    for i in range(T // 8):
        for j in range(H // 128):
            ref[i * (H // 128) + j] = value[8 * i : 8 * i + 8, 128 * j : 128 * j + 128]


def wide(ref):
    rows = [jnp.concatenate([ref[z * NX + x] for x in range(NX)], axis=1) for z in range(NZ)]
    return jnp.concatenate(rows, axis=0)


def quarter(shift):
    at = (lax.axis_index("samp") + shift) % NX
    return at, pl.ds(pl.multiple_of(at * FB, FB), FB)


def row_of(value):
    total = value[:, :128]
    for at in range(128, value.shape[1], 128):
        total = total + value[:, at : at + 128]
    return jnp.sum(total.T, axis=0, keepdims=True)


def rows_tile(rows):
    tile = jnp.concatenate(rows + [jnp.zeros((8 - len(rows), T), f32)], axis=0)
    return jnp.concatenate([tile, jnp.zeros((8, 128 - T), f32)], axis=1)


def columns_of(tile, count):
    turned = tile.T
    return [turned[:T, i : i + 1] for i in range(count)]


def scale0(tile):
    (square,) = columns_of(tile, 1)
    return lax.rsqrt(jnp.maximum(square, TINY))


def scale1(tile):
    overlap, square = columns_of(tile, 2)
    left = jnp.maximum(square - overlap * overlap, 1e-6 * square)
    return overlap, lax.rsqrt(jnp.maximum(left, TINY))


def tile_in(own_ref):
    return own_ref[TILES]


def first_kernel(a_hbm, b_hbm, out2_ref, out1_ref, out3_ref, both_ref, high_ref, low_ref, a_ref, b_ref, sems):
    copies = [pltpu.make_async_copy(b_hbm, b_ref, sems.at[PIECES])]
    for i in range(PIECES):
        rows = pl.ds(i * PIECE, PIECE)
        copies.append(pltpu.make_async_copy(a_hbm.at[rows, :], a_ref.at[i], sems.at[i]))
    for copy in copies:
        copy.start()
    copies[0].wait()
    high, low = split(b_ref[...])
    both = jnp.concatenate([high, low], axis=0)
    for i in range(PIECES):
        copies[i + 1].wait()
        a_high, a_low = split(a_ref[i])
        rows = slice(i * PIECE, (i + 1) * PIECE)
        high_ref[rows, :] = a_high
        low_ref[rows, :] = a_low
    both_ref[...] = both
    for shift, out_ref in zip(SENT, (out2_ref, out1_ref, out3_ref)):
        _, at = quarter(shift)
        put_half(out_ref, product(both, high, high_ref[:, at], low_ref[:, at]))


def first_last_kernel(both_ref, high_ref, low_ref, out_ref, high_t_ref, low_t_ref):
    both = both_ref[...]
    _, at = quarter(0)
    put_half(out_ref, product(both, both[:T], high_ref[:, at], low_ref[:, at]))
    for rows in (slice(i, i + PIECE) for i in range(0, S, PIECE)):
        for columns in (slice(i, i + PIECE) for i in range(0, F, PIECE)):
            high_t_ref[columns, rows] = high_ref[rows, columns].T
            low_t_ref[columns, rows] = low_ref[rows, columns].T


def first(a, b_t):
    anywhere = pl.BlockSpec(memory_space=pltpu.HBM)
    a = pltpu.with_memory_space_constraint(a, pltpu.HBM)
    b_t = pltpu.with_memory_space_constraint(b_t, pltpu.HBM)
    return pl.pallas_call(
        first_kernel,
        in_specs=[anywhere, anywhere],
        out_specs=[VMEM] * 6,
        out_shape=[
            *[pltpu.VMEM(*QUARTER) for _ in SENT],
            pltpu.VMEM((2 * T, S), bf16),
            pltpu.VMEM((S, F), bf16),
            pltpu.VMEM((S, F), bf16),
        ],
        scratch_shapes=[
            pltpu.VMEM((PIECES, PIECE, F), f32),
            pltpu.VMEM((T, S), f32),
            pltpu.SemaphoreType.DMA((PIECES + 1,)),
        ],
        compiler_params=pltpu.CompilerParams(vmem_limit_bytes=16 * 2**20),
        name="first",
    )(a, b_t)


def add_kernel(*refs):
    total = refs[0][...]
    for ref in refs[1:-1]:
        total = total + ref[...]
    refs[-1][...] = total


def lines_kernel(*refs):
    out_ref = refs[-1]
    for z in range(NZ):
        for j in range(out_ref.shape[1]):
            at = z * LINE + j if j < LINE else NZ * LINE
            total = refs[0][at]
            for ref in refs[1:-1]:
                total = total + ref[at]
            out_ref[z, j] = total


def sum_lines_kernel(in_ref, out_ref, *tile_refs):
    total = in_ref[0]
    for z in range(1, NZ):
        total = total + in_ref[z]
    block = jnp.concatenate([total[j] for j in range(LINE)], axis=1)
    for i in range(N):
        out_ref[i] = block
    for tile_ref in tile_refs:
        tile_ref[...] = total[LINE]


def sum_over_samp(parts):
    tiles = parts[0].shape[0] - NZ * LINE
    got = [lax.ppermute(parts[k], "samp", X_SHIFTS[k]) for k in (3, 1, 2)]
    (part,) = call(lines_kernel, [((NZ, LINE + tiles, 8, 128), f32)], "sum_x")(parts[0], *got)
    got = lax.all_to_all(part, "samp", 0, 0, axis_index_groups=GROUPS_Z)
    outs = [((N, TB, FB), f32)] + [((8, 128), f32)] * tiles
    part, *tile = call(sum_lines_kernel, outs, "sum_z")(got)
    return lax.all_to_all(part, "samp", 0, 0), *tile


def half_rows(own):
    core = lax.axis_index("feat") % NC
    at = core if own else 1 - core
    return pl.ds(pl.multiple_of(at * H, H), H)


def forward_send(value, scalars, high_ref, low_ref, send_ref, both_ref):
    high, low = split(value)
    both = jnp.concatenate([high, low], axis=0)
    both_ref[...] = both
    at = half_rows(False)
    put_half(send_ref, product(both, high, high_ref[:, at], low_ref[:, at]))
    send_ref[TILES] = rows_tile(scalars)


def send0_kernel(g_ref, high_ref, low_ref, send_ref, both_ref):
    g = wide(g_ref)
    forward_send(g, [row_of(g * g)], high_ref, low_ref, send_ref, both_ref)


def send1_kernel(g_ref, own0_ref, w_ref, high_ref, low_ref, send_ref, both_ref):
    e0 = wide(g_ref) * scale0(tile_in(own0_ref))
    w = wide(w_ref)
    forward_send(w, [row_of(e0 * w), row_of(w * w)], high_ref, low_ref, send_ref, both_ref)


def basis01(g_ref, own0_ref, w1_ref, own1_ref):
    e0 = wide(g_ref) * scale0(tile_in(own0_ref))
    overlap, scale = scale1(tile_in(own1_ref))
    return e0, (wide(w1_ref) - overlap * e0) * scale


def send2_kernel(
    g_ref, own0_ref, w1_ref, own1_ref, w_ref, tile_ref, high_ref, low_ref, send_ref, both_ref, q_ref
):
    e0, e1 = basis01(g_ref, own0_ref, w1_ref, own1_ref)
    overlap0, overlap1 = columns_of(tile_ref[...], 2)
    q = (wide(w_ref) - overlap0 * e0 - overlap1 * e1) * (1.0 / jnp.maximum(overlap1, TINY))
    q_ref[...] = q
    forward_send(q, [jnp.zeros((1, T), f32)], high_ref, low_ref, send_ref, both_ref)


def keep2_kernel(both_ref, g_ref, own0_ref, w1_ref, own1_ref, q_ref, high_ref, low_ref, keep_ref):
    both = both_ref[...]
    at = half_rows(True)
    put_half(keep_ref, product(both, both[:T], high_ref[:, at], low_ref[:, at]))
    e0, e1 = basis01(g_ref, own0_ref, w1_ref, own1_ref)
    q = q_ref[...]
    pairs = [(e0, e0), (e0, e1), (e0, q), (e1, e1), (e1, q), (q, q)]
    keep_ref[TILES] = rows_tile([row_of(left * right) for left, right in pairs])


def keep_kernel(both_ref, send_ref, high_ref, low_ref, keep_ref):
    both = both_ref[...]
    at = half_rows(True)
    put_half(keep_ref, product(both, both[:T], high_ref[:, at], low_ref[:, at]))
    keep_ref[TILES] = send_ref[TILES]


def sum_over_feat(kernel, args, turned, name):
    outs = [HALF, ((2 * T, F), bf16)]
    send, both = call(kernel, outs, name)(*args, *turned)
    got = lax.ppermute(send, "feat", CORE_SWAP)
    (keep,) = call(keep_kernel, [HALF], "keep")(both, send, *turned)
    return add_over_feat(keep, got)


def add_over_feat(keep, got):
    (part,) = call(add_kernel, [HALF], "add")(keep, got)
    got = [lax.ppermute(part, "feat", shift) for shift in Y_SHIFTS]
    (own,) = call(add_kernel, [HALF], "sum_y")(part, *got)
    return own, lax.ppermute(own, "feat", CORE_SWAP)


def image0(tile_ref, half0_ref):
    return half_in(half0_ref) * scale0(tile_in(tile_ref))


def image1(tile0_ref, half0_ref, tile1_ref, half1_ref):
    overlap, scale = scale1(tile_in(tile1_ref))
    return (half_in(half1_ref) - overlap * image0(tile0_ref, half0_ref)) * scale


def back_own(value, high_ref, low_ref, out_ref):
    high, low = split(value)
    both = jnp.concatenate([high, low], axis=0)
    rows = half_rows(True)
    for x in range(NX):
        at = slice(x * FB, (x + 1) * FB)
        out_ref[x] = product(both, high, high_ref[rows, at], low_ref[rows, at])


def back_quarter(shift, both, acc_ref, high_ref, low_ref, out_ref, *tiles):
    rows = half_rows(False)
    place, at = quarter(shift)
    put_half(out_ref, acc_ref[place] + product(both, both[:T], high_ref[rows, at], low_ref[rows, at]))
    for tile in tiles:
        out_ref[NZ * LINE] = tile


def back_others(value, acc_ref, high_ref, low_ref, out_refs, both_ref, *tiles):
    high, low = split(value)
    both = jnp.concatenate([high, low], axis=0)
    both_ref[...] = both
    for shift, out_ref in zip(SENT, out_refs):
        back_quarter(shift, both, acc_ref, high_ref, low_ref, out_ref, *tiles)


def back_mine_kernel(both_ref, acc_ref, high_ref, low_ref, *refs):
    tiles = [ref[...] for ref in refs[:-1]]
    back_quarter(0, both_ref[...], acc_ref, high_ref, low_ref, refs[-1], *tiles)


def back0_own_kernel(own0_ref, high_ref, low_ref, out_ref):
    back_own(image0(own0_ref, own0_ref), high_ref, low_ref, out_ref)


def back0_others_kernel(own0_ref, other0_ref, acc_ref, high_ref, low_ref, *refs):
    value = image0(own0_ref, other0_ref)
    back_others(value, acc_ref, high_ref, low_ref, refs[:-1], refs[-1])


def overlaps(u0, u1):
    return rows_tile([row_of(u0 * u1), row_of(u1 * u1)])


def back1_own_kernel(own0_ref, own1_ref, high_ref, low_ref, out_ref, tile_ref):
    u1 = image1(own0_ref, own0_ref, own1_ref, own1_ref)
    back_own(u1, high_ref, low_ref, out_ref)
    tile_ref[...] = overlaps(image0(own0_ref, own0_ref), u1)


def back1_others_kernel(
    own0_ref, other0_ref, own1_ref, other1_ref, tile_ref, acc_ref, high_ref, low_ref, *refs
):
    value = image1(own0_ref, other0_ref, own1_ref, other1_ref)
    tile = tile_ref[...] + overlaps(image0(own0_ref, other0_ref), value)
    refs[-1][...] = tile
    back_others(value, acc_ref, high_ref, low_ref, refs[:-2], refs[-2], tile)


def transposed(own_kernel, others_kernel, owns, halves, a_high, a_low, tiles, name):
    tile = [((8, 128), f32)] * tiles
    outs = [((NX, T, FB), f32)] + tile
    acc, *scalars = call(own_kernel, outs, name + "_own")(*owns, a_high, a_low)
    (count, *rest), dtype = QUARTER
    part = ((count + tiles, *rest), dtype)
    outs = [part] * len(SENT) + [((2 * T, H), bf16)] + tile
    args = (*halves, *scalars, acc, a_high, a_low)
    results = call(others_kernel, outs, name + "_others")(*args)
    sent, (both, *scalars) = results[: len(SENT)], results[len(SENT) :]
    (mine,) = call(back_mine_kernel, [part], name + "_mine")(both, acc, a_high, a_low, *scalars)
    return {0: mine, **dict(zip(SENT, sent))}


PAIRS = [(0, 0), (0, 1), (0, 2), (1, 1), (1, 2), (2, 2)]


def gram_rows(own, u_ref, half2_ref):
    at = half_rows(own)
    u = u_ref[0, :, at], u_ref[1, :, at], half_in(half2_ref)
    return rows_tile([row_of(u[i] * u[j]) for i, j in PAIRS])


def gram_own_kernel(u_ref, own2_ref, out_ref):
    out_ref[...] = gram_rows(True, u_ref, own2_ref)


def gram_kernel(u_ref, other2_ref, tile_ref, out_ref):
    tile = tile_ref[...] + gram_rows(False, u_ref, other2_ref)
    line = jnp.concatenate([tile[i : i + 1, :T] for i in range(8)], axis=1)
    for i in range(out_ref.shape[0]):
        out_ref[i] = line


def solve(gram, dots, square0, ridge):
    k00, k01, k02, k11, k12, k22 = [u + ridge * v for u, v in zip(gram, dots)]
    norm = jnp.sqrt(square0)
    r0, r1, r2 = dots[0] * norm, dots[1] * norm, dots[2] * norm
    inverse0 = 1.0 / jnp.maximum(k00, TINY)
    l10, l20 = k01 * inverse0, k02 * inverse0
    d1 = k11 - l10 * k01
    inverse1 = jnp.where(d1 > 1e-6 * k11, 1.0 / jnp.maximum(d1, TINY), 0.0)
    t = k12 - l20 * k01
    l21 = t * inverse1
    d2 = k22 - l20 * k02 - l21 * t
    inverse2 = jnp.where(d2 > 1e-6 * k22, 1.0 / jnp.maximum(d2, TINY), 0.0)
    z1 = r1 - l10 * r0
    z2 = r2 - l20 * r0 - l21 * z1
    c2 = z2 * inverse2
    c1 = z1 * inverse1 - l21 * c2
    c0 = r0 * inverse0 - l10 * c1 - l20 * c2
    return c0, c1, c2


def basis_kernel(g_ref, own0_ref, w1_ref, own1_ref, other0_ref, other1_ref, e_ref, u_ref):
    e_ref[0], e_ref[1] = basis01(g_ref, own0_ref, w1_ref, own1_ref)
    for own, half0_ref, half1_ref in ((True, own0_ref, own1_ref), (False, other0_ref, other1_ref)):
        at = half_rows(own)
        u_ref[0, :, at] = image0(own0_ref, half0_ref)
        u_ref[1, :, at] = image1(own0_ref, half0_ref, own1_ref, half1_ref)


def last_kernel(
    gram_ref, ridge_ref, b_ref, e_ref, q_ref, u_ref, own0_ref, own2_ref, other2_ref, x_ref, r_ref
):
    gram = gram_ref[0]
    for i in range(1, gram_ref.shape[0]):
        gram = gram + gram_ref[i]
    blank = jnp.zeros((1, 128 - T), f32)
    gram = [jnp.concatenate([gram[:, i * T : (i + 1) * T], blank], axis=1) for i in range(6)]
    dots = tile_in(own2_ref) + tile_in(other2_ref)
    row = lambda tile, i: tile[i : i + 1, :]
    coefficients = solve(
        gram,
        [row(dots, i) for i in range(6)],
        row(tile_in(own0_ref), 0),
        jnp.concatenate([ridge_ref[...], jnp.zeros((1, 128 - T), f32)], axis=1),
    )
    tile = jnp.concatenate(list(coefficients) + [jnp.zeros((5, 128), f32)], axis=0)
    c0, c1, c2 = columns_of(tile, 3)
    x_ref[...] = c0 * e_ref[0] + c1 * e_ref[1] + c2 * q_ref[...]
    for own, half2_ref in ((True, own2_ref), (False, other2_ref)):
        at = half_rows(own)
        r_ref[:, at] = b_ref[:, at] - c0 * u_ref[0, :, at] - c1 * u_ref[1, :, at] - c2 * half_in(half2_ref)


def last(*args):
    return pl.pallas_call(
        last_kernel,
        in_specs=[VMEM] * len(args),
        out_specs=[VMEM, VMEM],
        out_shape=[jax.ShapeDtypeStruct((T, F), f32), jax.ShapeDtypeStruct((T, S), f32)],
        compiler_params=pltpu.CompilerParams(vmem_limit_bytes=16 * 2**20),
        name="last",
    )(*args)


def per_device(features, targets, ridge):
    b_t = targets.T
    *sent, both, a_high, a_low = first(features, b_t)
    parts = dict(zip(SENT, sent))
    outs = [QUARTER, ((F, S), bf16), ((F, S), bf16)]
    parts[0], *turned = call(first_last_kernel, outs, "first_last")(both, a_high, a_low)
    (g,) = sum_over_samp(parts)
    own0, other0 = sum_over_feat(send0_kernel, (g,), turned, "send0")
    parts = transposed(
        back0_own_kernel, back0_others_kernel, (own0,), (own0, other0), a_high, a_low, 0, "back0"
    )
    (w1,) = sum_over_samp(parts)
    own1, other1 = sum_over_feat(send1_kernel, (g, own0, w1), turned, "send1")
    halves = (own0, other0, own1, other1)
    parts = transposed(
        back1_own_kernel, back1_others_kernel, (own0, own1), halves, a_high, a_low, 1, "back1"
    )
    w2, tile = sum_over_samp(parts)
    basis = (g, own0, w1, own1)
    outs = [HALF, ((2 * T, F), bf16), ((T, F), f32)]
    send, both, q = call(send2_kernel, outs, "send2")(*basis, w2, tile, *turned)
    got = lax.ppermute(send, "feat", CORE_SWAP)
    (keep,) = call(keep2_kernel, [HALF], "keep2")(both, *basis, q, *turned)
    own2, other2 = add_over_feat(keep, got)
    outs = [((2, T, F), f32), ((2, T, S), f32)]
    e, u = call(basis_kernel, outs, "basis")(*basis, other0, other1)
    (tile,) = call(gram_own_kernel, [((8, 128), f32)], "gram_own")(u, own2)
    (tiles,) = call(gram_kernel, [((N, 1, 8 * T), f32)], "gram")(u, other2, tile)
    gram = lax.all_to_all(tiles, "samp", 0, 0)
    x, r = last(gram, ridge.reshape(1, T), b_t, e, q, u, own0, own2, other2)
    return x.T, r.T


def solution(mesh):
    placed = (P("samp", "feat"), P("samp", None), P())
    return jax.shard_map(
        per_device,
        mesh=mesh,
        in_specs=placed,
        out_specs=(P("feat", None), P("samp", None)),
        check_vma=False,
    )
```

```python
import functools

import jax
import jax.numpy as jnp
from jax import lax
from jax.experimental import pallas as pl
from jax.experimental.pallas import tpu as pltpu
from jax.sharding import PartitionSpec as P

NZ, NX, NY, NC = 8, 4, 4, 2
Y_SHIFTS = [[(i, (i + NC * k) % (NY * NC)) for i in range(NY * NC)] for k in (3, 1, 2)]
X_SHIFTS = [[(i, i // NX * NX + (i + k) % NX) for i in range(NZ * NX)] for k in range(NX)]
GROUPS_Z = [[z * NX + x for z in range(NZ)] for x in range(NX)]
SENT = (2, 1, 3)
CORE_SWAP = [(i, i ^ 1) for i in range(NY * NC)]

T = 64
F = 2048
S = 1024
H = S // 2
N = NZ * NX
TB, FB = T // NZ, F // NX
TILES = (T // 8) * (H // 128)

f32, bf16 = jnp.float32, jnp.bfloat16
QUARTER = ((T // 8 * FB // 128, 8, 128), f32)
LINE = FB // 128
HALF = ((TILES + 1, 8, 128), f32)
TINY = 1e-35
VMEM = pl.BlockSpec(memory_space=pltpu.VMEM)
NN = (((1,), (0,)), ((), ()))
PIECES = 4
PIECE = S // PIECES


def call(kernel, outs, name, mib=10):
    shapes = [pltpu.VMEM(shape, dtype) for shape, dtype in outs]
    def run(*args):
        return pl.pallas_call(
            kernel,
            in_specs=[VMEM] * len(args),
            out_specs=[VMEM] * len(shapes),
            out_shape=shapes,
            compiler_params=pltpu.CompilerParams(vmem_limit_bytes=mib * 2**20),
            name=name,
        )(*args)
    return run


def split(value):
    high = value.astype(bf16)
    return high, (value - high.astype(f32)).astype(bf16)


def product(both, high, a_high, a_low):
    first = lax.dot_general(both, a_high, NN, preferred_element_type=f32)
    second = lax.dot_general(high, a_low, NN, preferred_element_type=f32)
    return first[:T] + first[T:] + second


def block_in(ref, z):
    return jnp.concatenate([ref[z * LINE + j] for j in range(LINE)], axis=1)


def half_in(ref):
    lines = [[ref[i * (H // 128) + j] for j in range(H // 128)] for i in range(T // 8)]
    return jnp.concatenate([jnp.concatenate(line, axis=1) for line in lines], axis=0)


def put_half(ref, value):
    for i in range(T // 8):
        for j in range(H // 128):
            ref[i * (H // 128) + j] = value[8 * i : 8 * i + 8, 128 * j : 128 * j + 128]


def wide(ref):
    rows = [jnp.concatenate([ref[z * NX + x] for x in range(NX)], axis=1) for z in range(NZ)]
    return jnp.concatenate(rows, axis=0)


def quarter(shift):
    at = (lax.axis_index("samp") + shift) % NX
    return at, pl.ds(pl.multiple_of(at * FB, FB), FB)


def row_of(value):
    total = value[:, :128]
    for at in range(128, value.shape[1], 128):
        total = total + value[:, at : at + 128]
    return jnp.sum(total.T, axis=0, keepdims=True)


def rows_tile(rows):
    tile = jnp.concatenate(rows + [jnp.zeros((8 - len(rows), T), f32)], axis=0)
    return jnp.concatenate([tile, jnp.zeros((8, 128 - T), f32)], axis=1)


def columns_of(tile, count):
    turned = tile.T
    return [turned[:T, i : i + 1] for i in range(count)]


def scale0(tile):
    (square,) = columns_of(tile, 1)
    return lax.rsqrt(jnp.maximum(square, TINY))


def scale1(tile):
    overlap, square = columns_of(tile, 2)
    left = jnp.maximum(square - overlap * overlap, 1e-6 * square)
    return overlap, lax.rsqrt(jnp.maximum(left, TINY))


def tile_in(own_ref):
    return own_ref[TILES]


def first_kernel(a_hbm, b_hbm, out2_ref, out1_ref, out3_ref, both_ref, high_ref, low_ref, a_ref, b_ref, sems):
    copies = [pltpu.make_async_copy(b_hbm, b_ref, sems.at[PIECES])]
    for i in range(PIECES):
        rows = pl.ds(i * PIECE, PIECE)
        copies.append(pltpu.make_async_copy(a_hbm.at[rows, :], a_ref.at[i], sems.at[i]))
    for copy in copies:
        copy.start()
    copies[0].wait()
    high, low = split(b_ref[...])
    both = jnp.concatenate([high, low], axis=0)
    for i in range(PIECES):
        copies[i + 1].wait()
        a_high, a_low = split(a_ref[i])
        rows = slice(i * PIECE, (i + 1) * PIECE)
        high_ref[rows, :] = a_high
        low_ref[rows, :] = a_low
    both_ref[...] = both
    for shift, out_ref in zip(SENT, (out2_ref, out1_ref, out3_ref)):
        _, at = quarter(shift)
        put_half(out_ref, product(both, high, high_ref[:, at], low_ref[:, at]))


def first_last_kernel(both_ref, high_ref, low_ref, out_ref, high_t_ref, low_t_ref):
    both = both_ref[...]
    _, at = quarter(0)
    put_half(out_ref, product(both, both[:T], high_ref[:, at], low_ref[:, at]))
    for rows in (slice(i, i + PIECE) for i in range(0, S, PIECE)):
        for columns in (slice(i, i + PIECE) for i in range(0, F, PIECE)):
            high_t_ref[columns, rows] = high_ref[rows, columns].T
            low_t_ref[columns, rows] = low_ref[rows, columns].T


def first(a, b_t):
    anywhere = pl.BlockSpec(memory_space=pltpu.HBM)
    a = pltpu.with_memory_space_constraint(a, pltpu.HBM)
    b_t = pltpu.with_memory_space_constraint(b_t, pltpu.HBM)
    return pl.pallas_call(
        first_kernel,
        in_specs=[anywhere, anywhere],
        out_specs=[VMEM] * 6,
        out_shape=[
            *[pltpu.VMEM(*QUARTER) for _ in SENT],
            pltpu.VMEM((2 * T, S), bf16),
            pltpu.VMEM((S, F), bf16),
            pltpu.VMEM((S, F), bf16),
        ],
        scratch_shapes=[
            pltpu.VMEM((PIECES, PIECE, F), f32),
            pltpu.VMEM((T, S), f32),
            pltpu.SemaphoreType.DMA((PIECES + 1,)),
        ],
        compiler_params=pltpu.CompilerParams(vmem_limit_bytes=16 * 2**20),
        name="first",
    )(a, b_t)


def add_kernel(*refs):
    total = refs[0][...]
    for ref in refs[1:-1]:
        total = total + ref[...]
    refs[-1][...] = total


def lines_kernel(*refs):
    out_ref = refs[-1]
    for z in range(NZ):
        for j in range(out_ref.shape[1]):
            at = z * LINE + j if j < LINE else NZ * LINE
            total = refs[0][at]
            for ref in refs[1:-1]:
                total = total + ref[at]
            out_ref[z, j] = total


def sum_lines_kernel(in_ref, out_ref, *tile_refs):
    total = in_ref[0]
    for z in range(1, NZ):
        total = total + in_ref[z]
    block = jnp.concatenate([total[j] for j in range(LINE)], axis=1)
    for i in range(N):
        out_ref[i] = block
    for tile_ref in tile_refs:
        tile_ref[...] = total[LINE]


def sum_over_samp(parts):
    tiles = parts[0].shape[0] - NZ * LINE
    got = [lax.ppermute(parts[k], "samp", X_SHIFTS[k]) for k in (3, 1, 2)]
    (part,) = call(lines_kernel, [((NZ, LINE + tiles, 8, 128), f32)], "sum_x")(parts[0], *got)
    got = lax.all_to_all(part, "samp", 0, 0, axis_index_groups=GROUPS_Z)
    outs = [((N, TB, FB), f32)] + [((8, 128), f32)] * tiles
    part, *tile = call(sum_lines_kernel, outs, "sum_z")(got)
    return lax.all_to_all(part, "samp", 0, 0), *tile


def half_rows(own):
    core = lax.axis_index("feat") % NC
    at = core if own else 1 - core
    return pl.ds(pl.multiple_of(at * H, H), H)


def forward_send(value, scalars, high_ref, low_ref, send_ref, both_ref):
    high, low = split(value)
    both = jnp.concatenate([high, low], axis=0)
    both_ref[...] = both
    at = half_rows(False)
    put_half(send_ref, product(both, high, high_ref[:, at], low_ref[:, at]))
    send_ref[TILES] = rows_tile(scalars)


def send0_kernel(g_ref, high_ref, low_ref, send_ref, both_ref):
    g = wide(g_ref)
    forward_send(g, [row_of(g * g)], high_ref, low_ref, send_ref, both_ref)


def send1_kernel(g_ref, own0_ref, w_ref, high_ref, low_ref, send_ref, both_ref):
    e0 = wide(g_ref) * scale0(tile_in(own0_ref))
    w = wide(w_ref)
    forward_send(w, [row_of(e0 * w), row_of(w * w)], high_ref, low_ref, send_ref, both_ref)


def basis01(g_ref, own0_ref, w1_ref, own1_ref):
    e0 = wide(g_ref) * scale0(tile_in(own0_ref))
    overlap, scale = scale1(tile_in(own1_ref))
    return e0, (wide(w1_ref) - overlap * e0) * scale


def send2_kernel(
    g_ref, own0_ref, w1_ref, own1_ref, w_ref, tile_ref, high_ref, low_ref, send_ref, both_ref, q_ref
):
    e0, e1 = basis01(g_ref, own0_ref, w1_ref, own1_ref)
    overlap0, overlap1 = columns_of(tile_ref[...], 2)
    q = (wide(w_ref) - overlap0 * e0 - overlap1 * e1) * (1.0 / jnp.maximum(overlap1, TINY))
    q_ref[...] = q
    forward_send(q, [jnp.zeros((1, T), f32)], high_ref, low_ref, send_ref, both_ref)


def keep2_kernel(both_ref, g_ref, own0_ref, w1_ref, own1_ref, q_ref, high_ref, low_ref, keep_ref):
    both = both_ref[...]
    at = half_rows(True)
    put_half(keep_ref, product(both, both[:T], high_ref[:, at], low_ref[:, at]))
    e0, e1 = basis01(g_ref, own0_ref, w1_ref, own1_ref)
    q = q_ref[...]
    pairs = [(e0, e0), (e0, e1), (e0, q), (e1, e1), (e1, q), (q, q)]
    keep_ref[TILES] = rows_tile([row_of(left * right) for left, right in pairs])


def keep_kernel(both_ref, send_ref, high_ref, low_ref, keep_ref):
    both = both_ref[...]
    at = half_rows(True)
    put_half(keep_ref, product(both, both[:T], high_ref[:, at], low_ref[:, at]))
    keep_ref[TILES] = send_ref[TILES]


def sum_over_feat(kernel, args, turned, name):
    outs = [HALF, ((2 * T, F), bf16)]
    send, both = call(kernel, outs, name)(*args, *turned)
    got = lax.ppermute(send, "feat", CORE_SWAP)
    (keep,) = call(keep_kernel, [HALF], "keep")(both, send, *turned)
    return add_over_feat(keep, got)


def add_over_feat(keep, got):
    (part,) = call(add_kernel, [HALF], "add")(keep, got)
    got = [lax.ppermute(part, "feat", shift) for shift in Y_SHIFTS]
    (own,) = call(add_kernel, [HALF], "sum_y")(part, *got)
    return own, lax.ppermute(own, "feat", CORE_SWAP)


def image0(tile_ref, half0_ref):
    return half_in(half0_ref) * scale0(tile_in(tile_ref))


def image1(tile0_ref, half0_ref, tile1_ref, half1_ref):
    overlap, scale = scale1(tile_in(tile1_ref))
    return (half_in(half1_ref) - overlap * image0(tile0_ref, half0_ref)) * scale


def back_own(value, high_ref, low_ref, out_ref):
    high, low = split(value)
    both = jnp.concatenate([high, low], axis=0)
    rows = half_rows(True)
    for x in range(NX):
        at = slice(x * FB, (x + 1) * FB)
        out_ref[x] = product(both, high, high_ref[rows, at], low_ref[rows, at])


def back_quarter(shift, both, acc_ref, high_ref, low_ref, out_ref, *tiles):
    rows = half_rows(False)
    place, at = quarter(shift)
    put_half(out_ref, acc_ref[place] + product(both, both[:T], high_ref[rows, at], low_ref[rows, at]))
    for tile in tiles:
        out_ref[NZ * LINE] = tile


def back_others(value, acc_ref, high_ref, low_ref, out_refs, both_ref, *tiles):
    high, low = split(value)
    both = jnp.concatenate([high, low], axis=0)
    both_ref[...] = both
    for shift, out_ref in zip(SENT, out_refs):
        back_quarter(shift, both, acc_ref, high_ref, low_ref, out_ref, *tiles)


def back_mine_kernel(both_ref, acc_ref, high_ref, low_ref, *refs):
    tiles = [ref[...] for ref in refs[:-1]]
    back_quarter(0, both_ref[...], acc_ref, high_ref, low_ref, refs[-1], *tiles)


def back0_own_kernel(own0_ref, high_ref, low_ref, out_ref):
    back_own(image0(own0_ref, own0_ref), high_ref, low_ref, out_ref)


def back0_others_kernel(own0_ref, other0_ref, acc_ref, high_ref, low_ref, *refs):
    value = image0(own0_ref, other0_ref)
    back_others(value, acc_ref, high_ref, low_ref, refs[:-1], refs[-1])


def overlaps(u0, u1):
    return rows_tile([row_of(u0 * u1), row_of(u1 * u1)])


def back1_own_kernel(own0_ref, own1_ref, high_ref, low_ref, out_ref, tile_ref):
    u1 = image1(own0_ref, own0_ref, own1_ref, own1_ref)
    back_own(u1, high_ref, low_ref, out_ref)
    tile_ref[...] = overlaps(image0(own0_ref, own0_ref), u1)


def back1_others_kernel(
    own0_ref, other0_ref, own1_ref, other1_ref, tile_ref, acc_ref, high_ref, low_ref, *refs
):
    value = image1(own0_ref, other0_ref, own1_ref, other1_ref)
    tile = tile_ref[...] + overlaps(image0(own0_ref, other0_ref), value)
    refs[-1][...] = tile
    back_others(value, acc_ref, high_ref, low_ref, refs[:-2], refs[-2], tile)


def transposed(own_kernel, others_kernel, owns, halves, a_high, a_low, tiles, name):
    tile = [((8, 128), f32)] * tiles
    outs = [((NX, T, FB), f32)] + tile
    acc, *scalars = call(own_kernel, outs, name + "_own")(*owns, a_high, a_low)
    (count, *rest), dtype = QUARTER
    part = ((count + tiles, *rest), dtype)
    outs = [part] * len(SENT) + [((2 * T, H), bf16)] + tile
    args = (*halves, *scalars, acc, a_high, a_low)
    results = call(others_kernel, outs, name + "_others")(*args)
    sent, (both, *scalars) = results[: len(SENT)], results[len(SENT) :]
    (mine,) = call(back_mine_kernel, [part], name + "_mine")(both, acc, a_high, a_low, *scalars)
    return {0: mine, **dict(zip(SENT, sent))}


PAIRS = [(0, 0), (0, 1), (0, 2), (1, 1), (1, 2), (2, 2)]


def gram_rows(own, u_ref, half2_ref):
    at = half_rows(own)
    u = u_ref[0, :, at], u_ref[1, :, at], half_in(half2_ref)
    return rows_tile([row_of(u[i] * u[j]) for i, j in PAIRS])


def gram_own_kernel(u_ref, own2_ref, out_ref):
    out_ref[...] = gram_rows(True, u_ref, own2_ref)


def gram_kernel(u_ref, other2_ref, tile_ref, out_ref):
    tile = tile_ref[...] + gram_rows(False, u_ref, other2_ref)
    line = jnp.concatenate([tile[i : i + 1, :T] for i in range(len(PAIRS))], axis=1)
    for i in range(out_ref.shape[0]):
        out_ref[i] = line


def solve(gram, dots, square0, ridge):
    k00, k01, k02, k11, k12, k22 = [u + ridge * v for u, v in zip(gram, dots)]
    norm = jnp.sqrt(square0)
    r0, r1, r2 = dots[0] * norm, dots[1] * norm, dots[2] * norm
    inverse0 = 1.0 / jnp.maximum(k00, TINY)
    l10, l20 = k01 * inverse0, k02 * inverse0
    d1 = k11 - l10 * k01
    inverse1 = jnp.where(d1 > 1e-6 * k11, 1.0 / jnp.maximum(d1, TINY), 0.0)
    t = k12 - l20 * k01
    l21 = t * inverse1
    d2 = k22 - l20 * k02 - l21 * t
    inverse2 = jnp.where(d2 > 1e-6 * k22, 1.0 / jnp.maximum(d2, TINY), 0.0)
    z1 = r1 - l10 * r0
    z2 = r2 - l20 * r0 - l21 * z1
    c2 = z2 * inverse2
    c1 = z1 * inverse1 - l21 * c2
    c0 = r0 * inverse0 - l10 * c1 - l20 * c2
    return c0, c1, c2


def basis_kernel(g_ref, own0_ref, w1_ref, own1_ref, other0_ref, other1_ref, e_ref, u_ref):
    e_ref[0], e_ref[1] = basis01(g_ref, own0_ref, w1_ref, own1_ref)
    for own, half0_ref, half1_ref in ((True, own0_ref, own1_ref), (False, other0_ref, other1_ref)):
        at = half_rows(own)
        u_ref[0, :, at] = image0(own0_ref, half0_ref)
        u_ref[1, :, at] = image1(own0_ref, half0_ref, own1_ref, half1_ref)


def last_kernel(
    gram_ref, ridge_ref, b_ref, e_ref, q_ref, u_ref, own0_ref, own2_ref, other2_ref, x_ref, r_ref
):
    gram = gram_ref[0]
    for i in range(1, gram_ref.shape[0]):
        gram = gram + gram_ref[i]
    blank = jnp.zeros((1, 128 - T), f32)
    gram = [jnp.concatenate([gram[:, i * T : (i + 1) * T], blank], axis=1) for i in range(6)]
    dots = tile_in(own2_ref) + tile_in(other2_ref)
    row = lambda tile, i: tile[i : i + 1, :]
    coefficients = solve(
        gram,
        [row(dots, i) for i in range(6)],
        row(tile_in(own0_ref), 0),
        jnp.concatenate([ridge_ref[...], jnp.zeros((1, 128 - T), f32)], axis=1),
    )
    tile = jnp.concatenate(list(coefficients) + [jnp.zeros((5, 128), f32)], axis=0)
    c0, c1, c2 = columns_of(tile, 3)
    x_ref[...] = c0 * e_ref[0] + c1 * e_ref[1] + c2 * q_ref[...]
    for own, half2_ref in ((True, own2_ref), (False, other2_ref)):
        at = half_rows(own)
        r_ref[:, at] = b_ref[:, at] - c0 * u_ref[0, :, at] - c1 * u_ref[1, :, at] - c2 * half_in(half2_ref)


def last(*args):
    return pl.pallas_call(
        last_kernel,
        in_specs=[VMEM] * len(args),
        out_specs=[VMEM, VMEM],
        out_shape=[jax.ShapeDtypeStruct((T, F), f32), jax.ShapeDtypeStruct((T, S), f32)],
        compiler_params=pltpu.CompilerParams(vmem_limit_bytes=16 * 2**20),
        name="last",
    )(*args)


def per_device(features, targets, ridge):
    b_t = targets.T
    *sent, both, a_high, a_low = first(features, b_t)
    parts = dict(zip(SENT, sent))
    outs = [QUARTER, ((F, S), bf16), ((F, S), bf16)]
    parts[0], *turned = call(first_last_kernel, outs, "first_last")(both, a_high, a_low)
    (g,) = sum_over_samp(parts)
    own0, other0 = sum_over_feat(send0_kernel, (g,), turned, "send0")
    parts = transposed(
        back0_own_kernel, back0_others_kernel, (own0,), (own0, other0), a_high, a_low, 0, "back0"
    )
    (w1,) = sum_over_samp(parts)
    own1, other1 = sum_over_feat(send1_kernel, (g, own0, w1), turned, "send1")
    halves = (own0, other0, own1, other1)
    parts = transposed(
        back1_own_kernel, back1_others_kernel, (own0, own1), halves, a_high, a_low, 1, "back1"
    )
    w2, tile = sum_over_samp(parts)
    basis = (g, own0, w1, own1)
    outs = [HALF, ((2 * T, F), bf16), ((T, F), f32)]
    send, both, q = call(send2_kernel, outs, "send2")(*basis, w2, tile, *turned)
    got = lax.ppermute(send, "feat", CORE_SWAP)
    (keep,) = call(keep2_kernel, [HALF], "keep2")(both, *basis, q, *turned)
    own2, other2 = add_over_feat(keep, got)
    outs = [((2, T, F), f32), ((2, T, S), f32)]
    e, u = call(basis_kernel, outs, "basis")(*basis, other0, other1)
    (tile,) = call(gram_own_kernel, [((8, 128), f32)], "gram_own")(u, own2)
    (tiles,) = call(gram_kernel, [((N, 1, len(PAIRS) * T), f32)], "gram")(u, other2, tile)
    gram = lax.all_to_all(tiles, "samp", 0, 0)
    x, r = last(gram, ridge.reshape(1, T), b_t, e, q, u, own0, own2, other2)
    return x.T, r.T


def solution(mesh):
    placed = (P("samp", "feat"), P("samp", None), P())
    return jax.shard_map(
        per_device,
        mesh=mesh,
        in_specs=placed,
        out_specs=(P("feat", None), P("samp", None)),
        check_vma=False,
    )
```
